32 devices in a mesh: shots: 2 (over y), freq: 4 (over x, core), tile: 4 (over z).
Axes of the slice: x: 2, y: 2, z: 4, core: 2. Of those that a mesh axis runs over, the one named last changes fastest.
Arguments:
- velocity: float32 [4, 96, 1024], P(None, 'tile', 'freq'), may hold values from 1.5 to 4.5
- src_cell: int32 [8192], P('shots'), parts along dimension 0, may hold values from 0 to 98303
- src_wave: float32 [2, 4, 8192], P(None, 'freq', 'shots'), parts along dimension 2, may hold values from -24 to 24
- rec_cell: int32 [32768], P('shots'), parts along dimension 0, may hold values from 0 to 98303
- rec_data: float32 [2, 4, 32768], P(None, 'freq', 'shots'), parts along dimension 2, may hold values from -24 to 24
Outputs:
- final_fields: float32 [4, 4, 2, 96, 1024], P('shots', 'freq', None, 'tile'), parts along dimension 0
- migrated_image: float32 [8, 96, 1024], P('shots', 'tile', 'freq'), parts along dimension 0
The draws below stay inside these ranges and needn't reach their ends.
There are 2 independent parts, one for each index of `shots`. The reference program is written for one: setup_inputs(seed, part) draws one part's arguments, and reference() takes and returns one part's arrays. A program takes and returns all parts, laid end to end along the dimension named above; an argument that names none is the same for every part. Nothing has to cross between parts.
Inputs may be any that keep to these rules, and one draw needn't show every extreme that they name: `src_cell`: each entry is a surface cell numbered row * 1024 + column; cells may repeat. `rec_cell`: each entry is a surface cell numbered row * 1024 + column; cells may repeat.
All inputs are finite; a program needn't handle non-finite values.
Results may differ from the reference program's by a relative error of at most 0.00002.
Values sent between devices are 32-bit elements; how exact they have to be, the bound alone decides.
A program may use at most 128 MiB of HBM per device.

```python
import math
import jax
import jax.numpy as jnp
from jax import lax

NY = 1024
STEPS = 4
PASSES = 5
NSRC = 4096
NREC = 16384
NX = 96
FREQS = 4


def set_ends(entries, own_key, low, top_value):
    extent = entries.shape
    index_at = [jax.random.randint(jax.random.fold_in(own_key, axis), (), 0, extent[axis]) for axis in range(len(extent))]
    entries = entries.at[tuple(index_at)].set(low)
    longest = extent.index(max(extent))
    index_at[longest] = (index_at[longest] + 1) % extent[longest]
    return entries.at[tuple(index_at)].set(top_value)


def block_scale(rng, dims, cuts, least, largest):
    def one(dim, parts):
        heights = jax.random.uniform(jax.random.fold_in(jax.random.fold_in(rng, 6), dim), (parts,), jnp.float32, least / len(cuts), largest / len(cuts))
        return jnp.repeat(jnp.exp(heights), dims[dim] // parts).reshape((-1,) + (1,) * (len(dims) - dim - 1))

    loudness = one(*cuts[0])
    for cut in cuts[1:]:
        loudness = loudness * one(*cut)
    return loudness


def noise(key, extent, scale, limit, pieces=(), kind=jnp.bfloat16):
    level = block_scale(key, extent, pieces, -0.22, 0.18) if pieces else 1.0
    drawn = jax.random.normal(key, extent, jnp.float32) * scale * level
    return jnp.minimum(jnp.maximum(drawn, -limit), limit).astype(kind)


def setup_inputs(seed: int = 0, part: int = 0) -> dict:
    arg_keys = jax.random.split(jax.random.key(seed), 6)
    part_splits = jax.random.split(jax.random.fold_in(arg_keys[5], part), 6)
    return {
        "velocity": jnp.clip(jnp.exp(math.log(4.5) - 1.0986123 * jax.random.uniform(arg_keys[0], (STEPS, NX, NY), jnp.float32) ** block_scale(arg_keys[0], (STEPS, NX, NY), ((1, 4), (2, 4)), -0.2, 0.2)), 1.5, 4.5),
        "src_cell": set_ends(jax.random.randint(part_splits[1], (NSRC,), 0, NX * NY), jax.random.fold_in(part_splits[1], 1), 0, (NX * NY) - 1).astype(jnp.int32),
        "src_wave": noise(part_splits[2], (2, FREQS, NSRC), 4.0, 24.0, ((1, 4),), jnp.float32),
        "rec_cell": set_ends(jax.random.randint(part_splits[3], (NREC,), 0, NX * NY), jax.random.fold_in(part_splits[3], 1), 0, (NX * NY) - 1).astype(jnp.int32),
        "rec_data": noise(part_splits[4], (2, FREQS, NREC), 4.0, 24.0, ((1, 4),), jnp.float32),
    }


term_weights = (0.30, 0.25, -0.15, 0.12, -0.10, 0.08)
phase_rates = (1.0, 0.8, 0.6, 0.45, 0.3, 0.2)
phase_unit = 0.25


def along_cols(values):
    blank_edge = jnp.zeros_like(values[..., :1])
    return jnp.concatenate([values[..., 1:], blank_edge], axis=-1) + jnp.concatenate([blank_edge, values[..., :-1]], axis=-1)


def mcclellan(padded):
    center = padded[..., 1:-1, :]
    across = padded[..., 2:, :] + padded[..., :-2, :]
    return -0.5 * center + 0.25 * across + 0.25 * along_cols(center) + 0.125 * along_cols(across)


def weighted(term, term_order, phase_base, conj_sign):
    real_coef = term_weights[term_order] * jnp.cos(phase_rates[term_order] * phase_base)
    imag_coef = conj_sign * (term_weights[term_order] * jnp.sin(phase_rates[term_order] * phase_base))
    term_real = term[..., 0, :, :]
    term_imag = term[..., 1, :, :]
    return jnp.stack([real_coef * term_real - imag_coef * term_imag, real_coef * term_imag + imag_coef * term_real], axis=-3)


def pad_rows(values):
    widths = [(0, 0)] * (values.ndim - 2) + [(1, 1), (0, 0)]
    return jnp.pad(values, widths)


def extrapolate(fields, phase_base, conj_sign):
    previous = fields
    summed = weighted(previous, 0, phase_base, conj_sign)
    current = mcclellan(pad_rows(previous))
    summed = summed + weighted(current, 1, phase_base, conj_sign)
    for term_order in range(2, PASSES + 1):
        following = 2.0 * mcclellan(pad_rows(current)) - previous
        summed = summed + weighted(following, term_order, phase_base, conj_sign)
        previous, current = current, following
    return summed


def inject(cell_ids, spectra):
    flat_field = jnp.zeros((2, NX * NY), jnp.float32).at[:, cell_ids].add(spectra)
    return flat_field.reshape(2, NX, NY)


def reference(velocity, src_cell, src_wave, rec_cell, rec_data):
    conj_sign = jnp.array([1.0, -1.0], jnp.float32).reshape(2, 1, 1)

    def one_frequency(image_sum, freq_index):
        fields = jnp.stack([inject(src_cell, src_wave[:, freq_index, :]), inject(rec_cell, rec_data[:, freq_index, :])])
        number = (freq_index + 1).astype(jnp.float32)
        depth_images = []
        for depth_step in range(STEPS):
            phase_base = number * phase_unit / velocity[depth_step]
            fields = extrapolate(fields, phase_base, conj_sign)
            depth_images.append(fields[0, 0] * fields[1, 0] + fields[0, 1] * fields[1, 1])
        return image_sum + jnp.stack(depth_images), fields

    empty_image = jnp.zeros((STEPS, NX, NY), jnp.float32)
    migrated_image, stacked = lax.scan(one_frequency, empty_image, jnp.arange(FREQS, dtype=jnp.int32))
    return jnp.transpose(stacked, (1, 0, 2, 3, 4)), migrated_image
```

```python
import functools
import math

import jax
import jax.numpy as jnp
from jax import lax
from jax.experimental import pallas as pl
from jax.experimental.pallas import tpu as pltpu
from jax.sharding import PartitionSpec as P

NY = 1024
STEPS = 4
PASSES = 5
LANES = 128
SUBLANES = 8

term_weights = (0.3, 0.25, -0.15, 0.12, -0.1, 0.08)
phase_unit = 0.25
slowest = 1.5

MESH = pl.DeviceIdType.MESH


def round_up(value, unit):
    return -(-value // unit) * unit


def series(angle, largest):
    square = angle * angle
    terms = 1
    while largest ** (2 * terms) / math.factorial(2 * terms) > 1e-9:
        terms += 1
    cos = sin = None
    for n in reversed(range(terms)):
        sign = -1.0 if n % 2 else 1.0
        even, odd = sign / math.factorial(2 * n), sign / math.factorial(2 * n + 1)
        cos = even if cos is None else cos * square + even
        sin = odd if sin is None else sin * square + odd
    return cos, sin * angle


def times(x, y):
    return x[0] * y[0] - x[1] * y[1], x[0] * y[1] + x[1] * y[0]


def double(x):
    twice = x[1] + x[1]
    return 1.0 - twice * x[1], twice * x[0]


def coefficients(kappa, largest):
    e15 = series(kappa * 0.15, largest * 0.15)
    e20 = series(kappa * 0.2, largest * 0.2)
    e30 = double(e15)
    e45 = times(e30, e15)
    e60 = double(e30)
    e80 = times(e60, e20)
    e100 = times(e80, e20)
    return [
        (w * c, w * s) for w, (c, s) in zip(term_weights, (e100, e80, e60, e45, e30, e20))
    ]


def kernel(
    freqs,
    tiles,
    velocity,
    src_cell,
    src_wave,
    rec_cell,
    rec_data,
    fields_out,
    image_out,
    speed,
    terms,
    sums,
    partial_image,
    image_in,
    speed_send,
    speed_recv,
    image_send,
    image_recv,
):
    f = lax.axis_index("freq")
    t = lax.axis_index("tile")
    rows = velocity.shape[1]
    own_cols = velocity.shape[2]
    blocks = NY // LANES
    halo = round_up(STEPS * PASSES, SUBLANES)
    window = rows + 2 * halo
    pad = SUBLANES
    has_above = t > 0
    has_below = t < tiles - 1

    groups = []
    for z in range(STEPS - 1):
        height = round_up(PASSES * (STEPS - 1 - z), SUBLANES)
        if groups and groups[-1][2] == height:
            groups[-1][1] = z + 1
        else:
            groups.append([z, z + 1, height])

    def other(step):
        return lax.rem(f + step, freqs)

    barrier = pltpu.get_barrier_semaphore()

    def greet(device):
        pl.semaphore_signal(barrier, inc=1, device_id=device, device_id_type=MESH)

    for step in range(1, freqs):
        greet({"freq": other(step)})

    @pl.when(has_above)
    def _():
        for step in range(freqs):
            greet({"freq": other(step), "tile": t - 1})

    @pl.when(has_below)
    def _():
        for step in range(freqs):
            greet({"freq": other(step), "tile": t + 1})

    neighbours = has_above.astype(jnp.int32) + has_below.astype(jnp.int32)
    pl.semaphore_wait(barrier, freqs - 1 + freqs * neighbours)

    def columns(owner):
        return pl.ds(pl.multiple_of(owner * own_cols, own_cols), own_cols)

    def level_copy(owner, target):
        return pltpu.make_async_remote_copy(
            src_ref=velocity,
            dst_ref=speed.at[:, pl.ds(halo, rows), columns(owner)],
            send_sem=speed_send.at[0, target, 0],
            recv_sem=speed_recv.at[0, owner, 0],
            device_id={"freq": target},
            device_id_type=MESH,
        )

    def down_copy(owner, target, g):
        low, high, height = groups[g]
        return pltpu.make_async_remote_copy(
            src_ref=velocity.at[pl.ds(low, high - low), pl.ds(rows - height, height)],
            dst_ref=speed.at[
                pl.ds(low, high - low), pl.ds(halo - height, height), columns(owner)
            ],
            send_sem=speed_send.at[1, target, g],
            recv_sem=speed_recv.at[1, owner, g],
            device_id={"freq": target, "tile": lax.rem(t + 1, tiles)},
            device_id_type=MESH,
        )

    def up_copy(owner, target, g):
        low, high, height = groups[g]
        return pltpu.make_async_remote_copy(
            src_ref=velocity.at[pl.ds(low, high - low), pl.ds(0, height)],
            dst_ref=speed.at[
                pl.ds(low, high - low), pl.ds(halo + rows, height), columns(owner)
            ],
            send_sem=speed_send.at[2, target, g],
            recv_sem=speed_recv.at[2, owner, g],
            device_id={"freq": target, "tile": lax.rem(t + tiles - 1, tiles)},
            device_id_type=MESH,
        )

    for step in range(1, freqs):
        level_copy(f, other(step)).start()

    @pl.when(has_below)
    def _():
        for g in range(len(groups)):
            for step in range(freqs):
                down_copy(f, other(step), g).start()

    @pl.when(has_above)
    def _():
        for g in range(len(groups)):
            for step in range(freqs):
                up_copy(f, other(step), g).start()

    speed[:, pl.ds(halo, rows), columns(f)] = velocity[...]

    @pl.when(jnp.logical_not(has_above))
    def _():
        speed[:, pl.ds(0, halo), :] = jnp.full((STEPS, halo, NY), 2.0, jnp.float32)

    @pl.when(jnp.logical_not(has_below))
    def _():
        speed[:, pl.ds(halo + rows, halo), :] = jnp.full((STEPS, halo, NY), 2.0, jnp.float32)

    for edge in (0, pad + window):
        terms[:, :, :, pl.ds(edge, pad), :] = jnp.zeros(
            (PASSES + 1, 4, blocks, pad, LANES), jnp.float32
        )

    first_row = t * rows - halo

    def inject(cells, data, field):
        count = cells.shape[1]
        chunk = math.gcd(count, 1024)
        sums[...] = jnp.zeros_like(sums)

        def add(i, carry):
            part = pl.ds(pl.multiple_of(i * chunk, chunk), chunk)
            cell = cells[:, part]
            row = (cell >> 10) - first_row
            col = cell & (NY - 1)
            inside = (row >= 0) & (row < window)
            place = jnp.where(inside, (col >> 7) * window + row, -1)
            lane = col & (LANES - 1)
            at_place = lax.broadcasted_iota(jnp.int32, (blocks * window, chunk), 0) == place
            at_lane = lax.broadcasted_iota(jnp.int32, (LANES, chunk), 0) == lane
            spread = []
            for c in range(2):
                value = data[c, :, part]
                head = value.astype(jnp.bfloat16).astype(jnp.float32)
                for piece in (head, value - head):
                    spread.append(jnp.where(at_lane, piece, 0.0).astype(jnp.bfloat16))
            one_hot = jnp.where(at_place, 1.0, 0.0).astype(jnp.bfloat16)
            sums[...] += lax.dot_general(
                one_hot,
                jnp.concatenate(spread, axis=0),
                (((1,), (1,)), ((), ())),
                preferred_element_type=jnp.float32,
            )
            return carry

        lax.fori_loop(0, count // chunk, add, 0)
        for c in range(2):
            for b in range(blocks):
                part = pl.ds(b * window, window)
                terms[0, 2 * field + c, b, pl.ds(pad, window), :] = (
                    sums[part, pl.ds(2 * c * LANES, LANES)]
                    + sums[part, pl.ds((2 * c + 1) * LANES, LANES)]
                )

    inject(src_cell, src_wave, 0)
    inject(rec_cell, rec_data, 1)

    for step in range(1, freqs):
        level_copy(other(step), other(step)).wait_recv()

    @pl.when(has_above)
    def _():
        for g in range(len(groups)):
            for owner in range(freqs):
                down_copy(owner, owner, g).wait_recv()

    @pl.when(has_below)
    def _():
        for g in range(len(groups)):
            for owner in range(freqs):
                up_copy(owner, owner, g).wait_recv()

    above_grid = jnp.where(has_above, 1.0, 0.0).astype(jnp.float32)
    below_grid = jnp.where(has_below, 1.0, 0.0).astype(jnp.float32)
    lane_index = lax.broadcasted_iota(jnp.int32, (SUBLANES, LANES), 1)
    at_first = lane_index == 0
    at_last = lane_index == LANES - 1
    number = (f + 1).astype(jnp.float32)
    largest = freqs * phase_unit / slowest

    def strips(margin):
        low = (halo - margin) // SUBLANES
        return range(low, round_up(halo + rows + margin, SUBLANES) // SUBLANES)

    def image_copy(z, owner, source):
        return pltpu.make_async_remote_copy(
            src_ref=partial_image.at[z, :, columns(owner)],
            dst_ref=image_in.at[z, source],
            send_sem=image_send.at[z, owner],
            recv_sem=image_recv.at[z, source],
            device_id={"freq": owner},
            device_id_type=MESH,
        )

    for z in range(STEPS):
        margin = PASSES * (STEPS - 1 - z)

        for k in range(1, PASSES + 1):

            def advance(plane, carry):
                for s in strips(margin + PASSES - k):
                    top = pad + s * SUBLANES
                    twice, tall = [], []
                    for b in range(blocks):
                        here = terms[k - 1, plane, b, pl.ds(top, SUBLANES), :]
                        over = terms[k - 1, plane, b, pl.ds(top - 1, SUBLANES), :]
                        under = terms[k - 1, plane, b, pl.ds(top + 1, SUBLANES), :]
                        twice.append(here + here)
                        tall.append(twice[b] + (over + under))
                    right = [pltpu.roll(v, 1, 1) for v in tall]
                    left = [pltpu.roll(v, LANES - 1, 1) for v in tall]
                    for b in range(blocks):
                        before = jnp.where(at_first, right[b - 1] if b else 0.0, right[b])
                        after = jnp.where(
                            at_last, left[b + 1] if b < blocks - 1 else 0.0, left[b]
                        )
                        wide = (tall[b] + tall[b]) + (before + after)
                        if k == 1:
                            new = 0.125 * wide - 0.5 * twice[b]
                        else:
                            new = (0.25 * wide - twice[b]) - terms[
                                k - 2, plane, b, pl.ds(top, SUBLANES), :
                            ]
                        if s * SUBLANES < halo:
                            new = new * above_grid
                        elif s * SUBLANES >= halo + rows:
                            new = new * below_grid
                        terms[k, plane, b, pl.ds(top, SUBLANES), :] = new
                return carry

            lax.fori_loop(0, 4, advance, 0)

        def combine(b, carry):
            lanes = pl.ds(pl.multiple_of(b * LANES, LANES), LANES)
            for s in strips(margin):
                top = pad + s * SUBLANES
                kappa = (number * phase_unit) / speed[z, pl.ds(s * SUBLANES, SUBLANES), lanes]
                total = [None] * 4
                for k, (real, imag) in enumerate(coefficients(kappa, largest)):
                    u = [terms[k, p, b, pl.ds(top, SUBLANES), :] for p in range(4)]
                    new = (
                        real * u[0] - imag * u[1],
                        real * u[1] + imag * u[0],
                        real * u[2] + imag * u[3],
                        real * u[3] - imag * u[2],
                    )
                    total = [n if o is None else o + n for o, n in zip(total, new)]
                own = s * SUBLANES - halo
                inside = 0 <= own < rows
                if z < STEPS - 1:
                    for p in range(4):
                        terms[0, p, b, pl.ds(top, SUBLANES), :] = total[p]
                else:
                    for p in range(4):
                        fields_out[p // 2, 0, p % 2, pl.ds(own, SUBLANES), lanes] = total[p]
                if inside:
                    partial_image[z, pl.ds(own, SUBLANES), lanes] = (
                        total[0] * total[2] + total[1] * total[3]
                    )
            return carry

        lax.fori_loop(0, blocks, combine, 0)
        for step in range(1, freqs):
            image_copy(z, other(step), f).start()

    for z in range(STEPS):
        whole = partial_image[z, :, columns(f)]
        for step in range(1, freqs):
            image_copy(z, f, other(step)).wait_recv()
            whole = whole + image_in[z, other(step)]
        image_out[z] = whole

    for z in range(STEPS):
        for step in range(1, freqs):
            image_copy(z, other(step), f).wait_send()
    for step in range(1, freqs):
        level_copy(f, other(step)).wait_send()

    @pl.when(has_below)
    def _():
        for g in range(len(groups)):
            for step in range(freqs):
                down_copy(f, other(step), g).wait_send()

    @pl.when(has_above)
    def _():
        for g in range(len(groups)):
            for step in range(freqs):
                up_copy(f, other(step), g).wait_send()


def body(freqs, tiles, velocity, src_cell, src_wave, rec_cell, rec_data):
    rows, own_cols = velocity.shape[1:]
    halo = round_up(STEPS * PASSES, SUBLANES)
    window = rows + 2 * halo
    blocks = NY // LANES
    assert src_wave.shape[1] == 1 and rows % SUBLANES == 0 and rows >= halo
    vmem = pl.BlockSpec(memory_space=pltpu.VMEM)
    return pl.pallas_call(
        functools.partial(kernel, freqs, tiles),
        out_shape=(
            jax.ShapeDtypeStruct((2, 1, 2, rows, NY), jnp.float32),
            jax.ShapeDtypeStruct((STEPS, rows, own_cols), jnp.float32),
        ),
        in_specs=[vmem] * 5,
        out_specs=(vmem, vmem),
        scratch_shapes=[
            pltpu.VMEM((STEPS, window, NY), jnp.float32),
            pltpu.VMEM((PASSES + 1, 4, blocks, window + 2 * SUBLANES, LANES), jnp.float32),
            pltpu.VMEM((blocks * window, 4 * LANES), jnp.float32),
            pltpu.VMEM((STEPS, rows, NY), jnp.float32),
            pltpu.VMEM((STEPS, freqs, rows, own_cols), jnp.float32),
            pltpu.SemaphoreType.DMA((3, freqs, STEPS)),
            pltpu.SemaphoreType.DMA((3, freqs, STEPS)),
            pltpu.SemaphoreType.DMA((STEPS, freqs)),
            pltpu.SemaphoreType.DMA((STEPS, freqs)),
        ],
        compiler_params=pltpu.CompilerParams(
            collective_id=0, has_side_effects=True, vmem_limit_bytes=40 * 1024 * 1024
        ),
    )(velocity, src_cell.reshape(1, -1), src_wave, rec_cell.reshape(1, -1), rec_data)


def solution(mesh):
    placed = (
        P(None, "tile", "freq"),
        P("shots"),
        P(None, "freq", "shots"),
        P("shots"),
        P(None, "freq", "shots"),
    )
    return jax.shard_map(
        functools.partial(body, mesh.shape["freq"], mesh.shape["tile"]),
        mesh=mesh,
        in_specs=placed,
        out_specs=(P("shots", "freq", None, "tile", None), P("shots", "tile", "freq")),
        check_vma=False,
    )
```

```python
import functools
import math

import jax
import jax.numpy as jnp
from jax import lax
from jax.experimental import pallas as pl
from jax.experimental.pallas import tpu as pltpu
from jax.sharding import PartitionSpec as P

NY = 1024
STEPS = 4
PASSES = 5
LANES = 128
SUBLANES = 8

term_weights = (0.3, 0.25, -0.15, 0.12, -0.1, 0.08)
phase_unit = 0.25
slowest = 1.5

MESH = pl.DeviceIdType.MESH


def round_up(value, unit):
    return -(-value // unit) * unit


def series(angle, largest):
    square = angle * angle
    terms = 1
    while largest ** (2 * terms) / math.factorial(2 * terms) > 1e-9:
        terms += 1
    cos = sin = None
    for n in reversed(range(terms)):
        sign = -1.0 if n % 2 else 1.0
        even, odd = sign / math.factorial(2 * n), sign / math.factorial(2 * n + 1)
        cos = even if cos is None else cos * square + even
        sin = odd if sin is None else sin * square + odd
    return cos, sin * angle


def times(x, y):
    return x[0] * y[0] - x[1] * y[1], x[0] * y[1] + x[1] * y[0]


def double(x):
    twice = x[1] + x[1]
    return 1.0 - twice * x[1], twice * x[0]


def coefficients(kappa, largest):
    e15 = series(kappa * 0.15, largest * 0.15)
    e20 = series(kappa * 0.2, largest * 0.2)
    e30 = double(e15)
    e45 = times(e30, e15)
    e60 = double(e30)
    e80 = times(e60, e20)
    e100 = times(e80, e20)
    return [
        (w * c, w * s) for w, (c, s) in zip(term_weights, (e100, e80, e60, e45, e30, e20))
    ]


def kernel(
    freqs,
    tiles,
    velocity,
    src_cell_in,
    src_wave_in,
    rec_cell_in,
    rec_data_in,
    fields_out,
    image_out,
    src_cell,
    src_wave,
    rec_cell,
    rec_data,
    speed,
    terms,
    sums,
    partial_image,
    image_in,
    speed_send,
    speed_recv,
    image_send,
    image_recv,
    local,
):
    f = lax.axis_index("freq")
    t = lax.axis_index("tile")
    rows = velocity.shape[1]
    own_cols = velocity.shape[2]
    blocks = NY // LANES
    reach = STEPS * PASSES
    halo = round_up(reach, SUBLANES)
    window = rows + 2 * halo
    pad = SUBLANES
    has_above = t > 0
    has_below = t < tiles - 1

    groups = []
    for z in range(STEPS - 1):
        height = round_up(PASSES * (STEPS - 1 - z), SUBLANES)
        if groups and groups[-1][2] == height:
            groups[-1][1] = z + 1
        else:
            groups.append([z, z + 1, height])

    def other(step):
        return lax.rem(f + step, freqs)

    def columns(owner):
        return pl.ds(pl.multiple_of(owner * own_cols, own_cols), own_cols)

    loads = [
        pltpu.make_async_copy(source, target, local.at[i])
        for i, (source, target) in enumerate(
            (
                (src_cell_in, src_cell),
                (src_wave_in, src_wave),
                (rec_cell_in, rec_cell),
                (rec_data_in, rec_data),
                (velocity, speed.at[:, pl.ds(halo, rows), columns(f)]),
            )
        )
    ]
    for load in loads:
        load.start()

    barrier = pltpu.get_barrier_semaphore()

    def greet(device):
        pl.semaphore_signal(barrier, inc=1, device_id=device, device_id_type=MESH)

    for step in range(1, freqs):
        greet({"freq": other(step)})

    @pl.when(has_above)
    def _():
        for step in range(freqs):
            greet({"freq": other(step), "tile": t - 1})

    @pl.when(has_below)
    def _():
        for step in range(freqs):
            greet({"freq": other(step), "tile": t + 1})

    neighbours = has_above.astype(jnp.int32) + has_below.astype(jnp.int32)
    pl.semaphore_wait(barrier, freqs - 1 + freqs * neighbours)

    def level_copy(owner, target):
        return pltpu.make_async_remote_copy(
            src_ref=velocity,
            dst_ref=speed.at[:, pl.ds(halo, rows), columns(owner)],
            send_sem=speed_send.at[0, target, 0],
            recv_sem=speed_recv.at[0, owner, 0],
            device_id={"freq": target},
            device_id_type=MESH,
        )

    def down_copy(owner, target, g):
        low, high, height = groups[g]
        return pltpu.make_async_remote_copy(
            src_ref=velocity.at[pl.ds(low, high - low), pl.ds(rows - height, height)],
            dst_ref=speed.at[
                pl.ds(low, high - low), pl.ds(halo - height, height), columns(owner)
            ],
            send_sem=speed_send.at[1, target, g],
            recv_sem=speed_recv.at[1, owner, g],
            device_id={"freq": target, "tile": lax.rem(t + 1, tiles)},
            device_id_type=MESH,
        )

    def up_copy(owner, target, g):
        low, high, height = groups[g]
        return pltpu.make_async_remote_copy(
            src_ref=velocity.at[pl.ds(low, high - low), pl.ds(0, height)],
            dst_ref=speed.at[
                pl.ds(low, high - low), pl.ds(halo + rows, height), columns(owner)
            ],
            send_sem=speed_send.at[2, target, g],
            recv_sem=speed_recv.at[2, owner, g],
            device_id={"freq": target, "tile": lax.rem(t + tiles - 1, tiles)},
            device_id_type=MESH,
        )

    for step in range(1, freqs):
        level_copy(f, other(step)).start()

    @pl.when(has_below)
    def _():
        for g in range(len(groups)):
            for step in range(freqs):
                down_copy(f, other(step), g).start()

    @pl.when(has_above)
    def _():
        for g in range(len(groups)):
            for step in range(freqs):
                up_copy(f, other(step), g).start()

    @pl.when(jnp.logical_not(has_above))
    def _():
        speed[:, pl.ds(0, halo), :] = jnp.full((STEPS, halo, NY), 2.0, jnp.float32)

    @pl.when(jnp.logical_not(has_below))
    def _():
        speed[:, pl.ds(halo + rows, halo), :] = jnp.full((STEPS, halo, NY), 2.0, jnp.float32)

    for edge in (0, pad + window):
        terms[:, :, :, pl.ds(edge, pad), :] = jnp.zeros(
            (PASSES + 1, 4, blocks, pad, LANES), jnp.float32
        )
    edge_rows = round_up(halo - reach, SUBLANES)
    for edge in (pad, pad + window - edge_rows):
        if edge_rows:
            terms[0, :, :, pl.ds(edge, edge_rows), :] = jnp.zeros(
                (4, blocks, edge_rows, LANES), jnp.float32
            )

    first_row = t * rows - reach
    height = round_up(rows + 2 * reach, SUBLANES)

    def inject(cells, data, field):
        count = cells.shape[1]
        chunk = math.gcd(count, 1024)
        sums[...] = jnp.zeros_like(sums)

        def add(i, carry):
            part = pl.ds(pl.multiple_of(i * chunk, chunk), chunk)
            cell = cells[:, part]
            row = (cell >> 10) - first_row
            col = cell & (NY - 1)
            inside = (row >= 0) & (row < height)
            place = jnp.where(inside, (col >> 7) * height + row, -1)
            lane = col & (LANES - 1)
            place, lane = place.astype(jnp.int16), lane.astype(jnp.int16)
            at_place = lax.broadcasted_iota(jnp.int16, (blocks * height, chunk), 0) == place
            at_lane = lax.broadcasted_iota(jnp.int16, (LANES, chunk), 0) == lane
            one, zero = jnp.bfloat16(1.0), jnp.bfloat16(0.0)
            spread = []
            for c in range(2):
                value = data[c, :, part]
                head = value.astype(jnp.bfloat16)
                rest = (value - head.astype(jnp.float32)).astype(jnp.bfloat16)
                for piece in (head, rest):
                    spread.append(jnp.where(at_lane, piece, zero))
            one_hot = jnp.where(at_place, one, zero)
            sums[...] += lax.dot_general(
                one_hot,
                jnp.concatenate(spread, axis=0),
                (((1,), (1,)), ((), ())),
                preferred_element_type=jnp.float32,
            )
            return carry

        lax.fori_loop(0, count // chunk, add, 0)
        for c in range(2):
            for b in range(blocks):
                part = pl.ds(b * height, height)
                terms[0, 2 * field + c, b, pl.ds(pad + halo - reach, height), :] = (
                    sums[part, pl.ds(2 * c * LANES, LANES)]
                    + sums[part, pl.ds((2 * c + 1) * LANES, LANES)]
                )

    loads[0].wait()
    loads[1].wait()
    inject(src_cell, src_wave, 0)
    loads[2].wait()
    loads[3].wait()
    inject(rec_cell, rec_data, 1)
    loads[4].wait()

    for step in range(1, freqs):
        level_copy(other(step), other(step)).wait_recv()

    @pl.when(has_above)
    def _():
        for g in range(len(groups)):
            for owner in range(freqs):
                down_copy(owner, owner, g).wait_recv()

    @pl.when(has_below)
    def _():
        for g in range(len(groups)):
            for owner in range(freqs):
                up_copy(owner, owner, g).wait_recv()

    above_grid = jnp.where(has_above, 1.0, 0.0).astype(jnp.float32)
    below_grid = jnp.where(has_below, 1.0, 0.0).astype(jnp.float32)
    lane_index = lax.broadcasted_iota(jnp.int32, (SUBLANES, LANES), 1)
    at_first = lane_index == 0
    at_last = lane_index == LANES - 1
    number = (f + 1).astype(jnp.float32)
    largest = freqs * phase_unit / slowest

    def strips(margin):
        low = (halo - margin) // SUBLANES
        return range(low, round_up(halo + rows + margin, SUBLANES) // SUBLANES)

    def image_copy(z, owner, source):
        return pltpu.make_async_remote_copy(
            src_ref=partial_image.at[z, :, columns(owner)],
            dst_ref=image_in.at[z, source],
            send_sem=image_send.at[z, owner],
            recv_sem=image_recv.at[z, source],
            device_id={"freq": owner},
            device_id_type=MESH,
        )

    for z in range(STEPS):
        margin = PASSES * (STEPS - 1 - z)

        for k in range(1, PASSES + 1):

            def advance(plane, carry):
                for s in strips(margin + PASSES - k):
                    top = pad + s * SUBLANES
                    twice, tall = [], []
                    for b in range(blocks):
                        here = terms[k - 1, plane, b, pl.ds(top, SUBLANES), :]
                        over = terms[k - 1, plane, b, pl.ds(top - 1, SUBLANES), :]
                        under = terms[k - 1, plane, b, pl.ds(top + 1, SUBLANES), :]
                        twice.append(here + here)
                        tall.append(twice[b] + (over + under))
                    right = [pltpu.roll(v, 1, 1) for v in tall]
                    left = [pltpu.roll(v, LANES - 1, 1) for v in tall]
                    for b in range(blocks):
                        before = jnp.where(at_first, right[b - 1] if b else 0.0, right[b])
                        after = jnp.where(
                            at_last, left[b + 1] if b < blocks - 1 else 0.0, left[b]
                        )
                        wide = (tall[b] + tall[b]) + (before + after)
                        if k == 1:
                            new = 0.125 * wide - 0.5 * twice[b]
                        else:
                            new = (0.25 * wide - twice[b]) - terms[
                                k - 2, plane, b, pl.ds(top, SUBLANES), :
                            ]
                        if s * SUBLANES < halo:
                            new = new * above_grid
                        elif s * SUBLANES >= halo + rows:
                            new = new * below_grid
                        terms[k, plane, b, pl.ds(top, SUBLANES), :] = new
                return carry

            lax.fori_loop(0, 4, advance, 0)

        def combine(b, carry):
            lanes = pl.ds(pl.multiple_of(b * LANES, LANES), LANES)
            for s in strips(margin):
                top = pad + s * SUBLANES
                kappa = (number * phase_unit) / speed[z, pl.ds(s * SUBLANES, SUBLANES), lanes]
                total = [None] * 4
                for k, (real, imag) in enumerate(coefficients(kappa, largest)):
                    u = [terms[k, p, b, pl.ds(top, SUBLANES), :] for p in range(4)]
                    new = (
                        real * u[0] - imag * u[1],
                        real * u[1] + imag * u[0],
                        real * u[2] + imag * u[3],
                        real * u[3] - imag * u[2],
                    )
                    total = [n if o is None else o + n for o, n in zip(total, new)]
                own = s * SUBLANES - halo
                inside = 0 <= own < rows
                if z < STEPS - 1:
                    for p in range(4):
                        terms[0, p, b, pl.ds(top, SUBLANES), :] = total[p]
                else:
                    for p in range(4):
                        fields_out[p // 2, 0, p % 2, pl.ds(own, SUBLANES), lanes] = total[p]
                if inside:
                    partial_image[z, pl.ds(own, SUBLANES), lanes] = (
                        total[0] * total[2] + total[1] * total[3]
                    )
            return carry

        lax.fori_loop(0, blocks, combine, 0)
        for step in range(1, freqs):
            image_copy(z, other(step), f).start()

    for z in range(STEPS):
        whole = partial_image[z, :, columns(f)]
        for step in range(1, freqs):
            image_copy(z, f, other(step)).wait_recv()
            whole = whole + image_in[z, other(step)]
        image_out[z] = whole

    for z in range(STEPS):
        for step in range(1, freqs):
            image_copy(z, other(step), f).wait_send()
    for step in range(1, freqs):
        level_copy(f, other(step)).wait_send()

    @pl.when(has_below)
    def _():
        for g in range(len(groups)):
            for step in range(freqs):
                down_copy(f, other(step), g).wait_send()

    @pl.when(has_above)
    def _():
        for g in range(len(groups)):
            for step in range(freqs):
                up_copy(f, other(step), g).wait_send()


def body(freqs, tiles, velocity, src_cell, src_wave, rec_cell, rec_data):
    rows, own_cols = velocity.shape[1:]
    halo = round_up(STEPS * PASSES, SUBLANES)
    window = rows + 2 * halo
    height = round_up(rows + 2 * STEPS * PASSES, SUBLANES)
    nsrc, nrec = src_cell.shape[0], rec_cell.shape[0]
    blocks = NY // LANES
    assert src_wave.shape[1] == 1 and rows % SUBLANES == 0 and rows >= halo
    vmem = pl.BlockSpec(memory_space=pltpu.VMEM)
    return pl.pallas_call(
        functools.partial(kernel, freqs, tiles),
        out_shape=(
            jax.ShapeDtypeStruct((2, 1, 2, rows, NY), jnp.float32),
            jax.ShapeDtypeStruct((STEPS, rows, own_cols), jnp.float32),
        ),
        in_specs=[pl.BlockSpec(memory_space=pltpu.HBM)] * 5,
        out_specs=(vmem, vmem),
        scratch_shapes=[
            pltpu.VMEM((1, nsrc), jnp.int32),
            pltpu.VMEM((2, 1, nsrc), jnp.float32),
            pltpu.VMEM((1, nrec), jnp.int32),
            pltpu.VMEM((2, 1, nrec), jnp.float32),
            pltpu.VMEM((STEPS, window, NY), jnp.float32),
            pltpu.VMEM((PASSES + 1, 4, blocks, window + 2 * SUBLANES, LANES), jnp.float32),
            pltpu.VMEM((blocks * height, 4 * LANES), jnp.float32),
            pltpu.VMEM((STEPS, rows, NY), jnp.float32),
            pltpu.VMEM((STEPS, freqs, rows, own_cols), jnp.float32),
            pltpu.SemaphoreType.DMA((3, freqs, STEPS)),
            pltpu.SemaphoreType.DMA((3, freqs, STEPS)),
            pltpu.SemaphoreType.DMA((STEPS, freqs)),
            pltpu.SemaphoreType.DMA((STEPS, freqs)),
            pltpu.SemaphoreType.DMA((5,)),
        ],
        compiler_params=pltpu.CompilerParams(
            collective_id=0, has_side_effects=True, vmem_limit_bytes=60 * 1024 * 1024
        ),
    )(velocity, src_cell.reshape(1, -1), src_wave, rec_cell.reshape(1, -1), rec_data)


def solution(mesh):
    placed = (
        P(None, "tile", "freq"),
        P("shots"),
        P(None, "freq", "shots"),
        P("shots"),
        P(None, "freq", "shots"),
    )
    return jax.shard_map(
        functools.partial(body, mesh.shape["freq"], mesh.shape["tile"]),
        mesh=mesh,
        in_specs=placed,
        out_specs=(P("shots", "freq", None, "tile", None), P("shots", "tile", "freq")),
        check_vma=False,
    )
```

```python
import functools
import math

import jax
import jax.numpy as jnp
from jax import lax
from jax.experimental import pallas as pl
from jax.experimental.pallas import tpu as pltpu
from jax.sharding import PartitionSpec as P

NY = 1024
STEPS = 4
PASSES = 5
LANES = 128
SUBLANES = 8

term_weights = (0.3, 0.25, -0.15, 0.12, -0.1, 0.08)
phase_unit = 0.25
slowest = 1.5

MESH = pl.DeviceIdType.MESH


def round_up(value, unit):
    return -(-value // unit) * unit


def series(angle, largest):
    square = angle * angle
    terms = 1
    while largest ** (2 * terms) / math.factorial(2 * terms) > 1e-9:
        terms += 1
    cos = sin = None
    for n in reversed(range(terms)):
        sign = -1.0 if n % 2 else 1.0
        even, odd = sign / math.factorial(2 * n), sign / math.factorial(2 * n + 1)
        cos = even if cos is None else cos * square + even
        sin = odd if sin is None else sin * square + odd
    return cos, sin * angle


def times(x, y):
    return x[0] * y[0] - x[1] * y[1], x[0] * y[1] + x[1] * y[0]


def double(x):
    twice = x[1] + x[1]
    return 1.0 - twice * x[1], twice * x[0]


def coefficients(kappa, largest):
    e15 = series(kappa * 0.15, largest * 0.15)
    e20 = series(kappa * 0.2, largest * 0.2)
    e30 = double(e15)
    e45 = times(e30, e15)
    e60 = double(e30)
    e80 = times(e60, e20)
    e100 = times(e80, e20)
    return [
        (w * c, w * s) for w, (c, s) in zip(term_weights, (e100, e80, e60, e45, e30, e20))
    ]


def kernel(
    freqs,
    tiles,
    velocity,
    src_cell_in,
    src_fold_in,
    src_wave_in,
    rec_cell_in,
    rec_fold_in,
    rec_data_in,
    fields_out,
    image_out,
    src_cell,
    src_fold,
    src_wave,
    rec_cell,
    rec_fold,
    rec_data,
    speed,
    terms,
    sums,
    partial_image,
    image_in,
    speed_send,
    speed_recv,
    image_send,
    image_recv,
    local,
):
    f = lax.axis_index("freq")
    t = lax.axis_index("tile")
    rows = velocity.shape[1]
    own_cols = velocity.shape[2]
    blocks = NY // LANES
    reach = STEPS * PASSES
    halo = round_up(reach, SUBLANES)
    window = rows + 2 * halo
    pad = SUBLANES
    has_above = t > 0
    has_below = t < tiles - 1

    groups = []
    for z in range(STEPS - 1):
        height = round_up(PASSES * (STEPS - 1 - z), SUBLANES)
        if groups and groups[-1][2] == height:
            groups[-1][1] = z + 1
        else:
            groups.append([z, z + 1, height])

    def other(step):
        return lax.rem(f + step, freqs)

    def columns(owner):
        return pl.ds(pl.multiple_of(owner * own_cols, own_cols), own_cols)

    loads = [
        pltpu.make_async_copy(source, target, local.at[i])
        for i, (source, target) in enumerate(
            (
                (src_cell_in, src_cell),
                (src_fold_in, src_fold),
                (src_wave_in, src_wave),
                (rec_cell_in, rec_cell),
                (rec_fold_in, rec_fold),
                (rec_data_in, rec_data),
                (velocity, speed.at[:, pl.ds(halo, rows), columns(f)]),
            )
        )
    ]
    for load in loads:
        load.start()

    barrier = pltpu.get_barrier_semaphore()

    def greet(device):
        pl.semaphore_signal(barrier, inc=1, device_id=device, device_id_type=MESH)

    for step in range(1, freqs):
        greet({"freq": other(step)})

    @pl.when(has_above)
    def _():
        for step in range(freqs):
            greet({"freq": other(step), "tile": t - 1})

    @pl.when(has_below)
    def _():
        for step in range(freqs):
            greet({"freq": other(step), "tile": t + 1})

    neighbours = has_above.astype(jnp.int32) + has_below.astype(jnp.int32)
    pl.semaphore_wait(barrier, freqs - 1 + freqs * neighbours)

    def level_copy(owner, target):
        return pltpu.make_async_remote_copy(
            src_ref=velocity,
            dst_ref=speed.at[:, pl.ds(halo, rows), columns(owner)],
            send_sem=speed_send.at[0, target, 0],
            recv_sem=speed_recv.at[0, owner, 0],
            device_id={"freq": target},
            device_id_type=MESH,
        )

    def down_copy(owner, target, g):
        low, high, height = groups[g]
        return pltpu.make_async_remote_copy(
            src_ref=velocity.at[pl.ds(low, high - low), pl.ds(rows - height, height)],
            dst_ref=speed.at[
                pl.ds(low, high - low), pl.ds(halo - height, height), columns(owner)
            ],
            send_sem=speed_send.at[1, target, g],
            recv_sem=speed_recv.at[1, owner, g],
            device_id={"freq": target, "tile": lax.rem(t + 1, tiles)},
            device_id_type=MESH,
        )

    def up_copy(owner, target, g):
        low, high, height = groups[g]
        return pltpu.make_async_remote_copy(
            src_ref=velocity.at[pl.ds(low, high - low), pl.ds(0, height)],
            dst_ref=speed.at[
                pl.ds(low, high - low), pl.ds(halo + rows, height), columns(owner)
            ],
            send_sem=speed_send.at[2, target, g],
            recv_sem=speed_recv.at[2, owner, g],
            device_id={"freq": target, "tile": lax.rem(t + tiles - 1, tiles)},
            device_id_type=MESH,
        )

    for step in range(1, freqs):
        level_copy(f, other(step)).start()

    @pl.when(has_below)
    def _():
        for g in range(len(groups)):
            for step in range(freqs):
                down_copy(f, other(step), g).start()

    @pl.when(has_above)
    def _():
        for g in range(len(groups)):
            for step in range(freqs):
                up_copy(f, other(step), g).start()

    @pl.when(jnp.logical_not(has_above))
    def _():
        speed[:, pl.ds(0, halo), :] = jnp.full((STEPS, halo, NY), 2.0, jnp.float32)

    @pl.when(jnp.logical_not(has_below))
    def _():
        speed[:, pl.ds(halo + rows, halo), :] = jnp.full((STEPS, halo, NY), 2.0, jnp.float32)

    for edge in (0, pad + window):
        terms[:, :, :, pl.ds(edge, pad), :] = jnp.zeros(
            (PASSES + 1, 4, blocks, pad, LANES), jnp.float32
        )
    edge_rows = round_up(halo - reach, SUBLANES)
    for edge in (pad, pad + window - edge_rows):
        if edge_rows:
            terms[0, :, :, pl.ds(edge, edge_rows), :] = jnp.zeros(
                (4, blocks, edge_rows, LANES), jnp.float32
            )

    first_row = t * rows - reach
    height = round_up(rows + 2 * reach, SUBLANES)
    wide = 2 * LANES
    places = NY // wide * height

    def inject(cells, fold, data, field):
        count = cells.shape[1]
        chunk = math.gcd(count, 2048)
        folds = chunk // LANES
        sums[...] = jnp.zeros_like(sums)

        def add(i, carry):
            part = pl.ds(pl.multiple_of(i * chunk, chunk), chunk)
            cell = cells[:, part]
            row = (cell >> 10) - first_row
            col = cell & (NY - 1)
            inside = (row >= 0) & (row < height)
            place = jnp.where(inside, (col >> 8) * height + row, -1).astype(jnp.int16)
            at_place = lax.broadcasted_iota(jnp.int16, (places, chunk), 0) == place
            zero = jnp.bfloat16(0.0)
            spread = []
            for c in range(2):
                value = data[c, :, part]
                head = value.astype(jnp.bfloat16)
                rest = (value - head.astype(jnp.float32)).astype(jnp.bfloat16)
                for piece in (head, rest):
                    spread.append(jnp.where(at_place, piece, zero))
            lane = fold[pl.ds(pl.multiple_of(i * folds, folds), folds), :] & (wide - 1)
            lane = lane.T
            lanes = lax.broadcasted_iota(jnp.int32, (LANES, wide), 1)
            one_hot = [
                jnp.where(lanes == lane[:, q : q + 1], 1.0, 0.0).astype(jnp.bfloat16)
                for q in range(folds)
            ]
            sums[...] += jnp.dot(
                jnp.concatenate(spread, axis=0),
                jnp.concatenate(one_hot, axis=0),
                preferred_element_type=jnp.float32,
            )
            return carry

        lax.fori_loop(0, count // chunk, add, 0)
        for c in range(2):
            for b in range(blocks):
                top = 2 * c * places + b // 2 * height
                half = pl.ds(b % 2 * LANES, LANES)
                terms[0, 2 * field + c, b, pl.ds(pad + halo - reach, height), :] = (
                    sums[pl.ds(top, height), half] + sums[pl.ds(top + places, height), half]
                )

    for load in loads[:3]:
        load.wait()
    inject(src_cell, src_fold, src_wave, 0)
    for load in loads[3:6]:
        load.wait()
    inject(rec_cell, rec_fold, rec_data, 1)
    loads[6].wait()

    for step in range(1, freqs):
        level_copy(other(step), other(step)).wait_recv()

    @pl.when(has_above)
    def _():
        for g in range(len(groups)):
            for owner in range(freqs):
                down_copy(owner, owner, g).wait_recv()

    @pl.when(has_below)
    def _():
        for g in range(len(groups)):
            for owner in range(freqs):
                up_copy(owner, owner, g).wait_recv()

    above_grid = jnp.where(has_above, 1.0, 0.0).astype(jnp.float32)
    below_grid = jnp.where(has_below, 1.0, 0.0).astype(jnp.float32)
    lane_index = lax.broadcasted_iota(jnp.int32, (SUBLANES, LANES), 1)
    at_first = lane_index == 0
    at_last = lane_index == LANES - 1
    number = (f + 1).astype(jnp.float32)
    largest = freqs * phase_unit / slowest

    def strips(margin):
        low = (halo - margin) // SUBLANES
        return range(low, round_up(halo + rows + margin, SUBLANES) // SUBLANES)

    def image_copy(z, owner, source):
        return pltpu.make_async_remote_copy(
            src_ref=partial_image.at[z, :, columns(owner)],
            dst_ref=image_in.at[z, source],
            send_sem=image_send.at[z, owner],
            recv_sem=image_recv.at[z, source],
            device_id={"freq": owner},
            device_id_type=MESH,
        )

    for z in range(STEPS):
        margin = PASSES * (STEPS - 1 - z)

        for k in range(1, PASSES + 1):

            def advance(field, carry):
                base = lax.div(field, 2)
                for plane, s in [(2 * field + c, s) for c in range(2) for s in strips(margin + PASSES - k)]:
                    top = pad + s * SUBLANES
                    twice, tall = [], []
                    for b in range(blocks):
                        here = terms[k - 1, plane, b, pl.ds(top, SUBLANES), :]
                        over = terms[k - 1, plane, b, pl.ds(base + (top - 1), SUBLANES), :]
                        under = terms[k - 1, plane, b, pl.ds(base + (top + 1), SUBLANES), :]
                        twice.append(here + here)
                        tall.append(twice[b] + (over + under))
                    right = [pltpu.roll(v, 1, 1) for v in tall]
                    left = [pltpu.roll(v, LANES - 1, 1) for v in tall]
                    for b in range(blocks):
                        before = jnp.where(at_first, right[b - 1] if b else 0.0, right[b])
                        after = jnp.where(
                            at_last, left[b + 1] if b < blocks - 1 else 0.0, left[b]
                        )
                        across = (tall[b] + tall[b]) + (before + after)
                        if k == 1:
                            new = 0.125 * across - 0.5 * twice[b]
                        else:
                            new = (0.25 * across - twice[b]) - terms[
                                k - 2, plane, b, pl.ds(top, SUBLANES), :
                            ]
                        if s * SUBLANES < halo:
                            new = new * above_grid
                        elif s * SUBLANES >= halo + rows:
                            new = new * below_grid
                        terms[k, plane, b, pl.ds(top, SUBLANES), :] = new
                return carry

            lax.fori_loop(0, 2, advance, 0)

        def combine(b, carry):
            lanes = pl.ds(pl.multiple_of(b * LANES, LANES), LANES)
            for s in strips(margin):
                top = pad + s * SUBLANES
                kappa = (number * phase_unit) / speed[z, pl.ds(s * SUBLANES, SUBLANES), lanes]
                total = [None] * 4
                for k, (real, imag) in enumerate(coefficients(kappa, largest)):
                    u = [terms[k, p, b, pl.ds(top, SUBLANES), :] for p in range(4)]
                    new = (
                        real * u[0] - imag * u[1],
                        real * u[1] + imag * u[0],
                        real * u[2] + imag * u[3],
                        real * u[3] - imag * u[2],
                    )
                    total = [n if o is None else o + n for o, n in zip(total, new)]
                own = s * SUBLANES - halo
                inside = 0 <= own < rows
                if z < STEPS - 1:
                    for p in range(4):
                        terms[0, p, b, pl.ds(top, SUBLANES), :] = total[p]
                else:
                    for p in range(4):
                        fields_out[p // 2, 0, p % 2, pl.ds(own, SUBLANES), lanes] = total[p]
                if inside:
                    partial_image[z, pl.ds(own, SUBLANES), lanes] = (
                        total[0] * total[2] + total[1] * total[3]
                    )
            return carry

        lax.fori_loop(0, blocks, combine, 0)
        for step in range(1, freqs):
            image_copy(z, other(step), f).start()

    for z in range(STEPS):
        whole = partial_image[z, :, columns(f)]
        for step in range(1, freqs):
            image_copy(z, f, other(step)).wait_recv()
            whole = whole + image_in[z, other(step)]
        image_out[z] = whole

    for z in range(STEPS):
        for step in range(1, freqs):
            image_copy(z, other(step), f).wait_send()
    for step in range(1, freqs):
        level_copy(f, other(step)).wait_send()

    @pl.when(has_below)
    def _():
        for g in range(len(groups)):
            for step in range(freqs):
                down_copy(f, other(step), g).wait_send()

    @pl.when(has_above)
    def _():
        for g in range(len(groups)):
            for step in range(freqs):
                up_copy(f, other(step), g).wait_send()


def body(freqs, tiles, velocity, src_cell, src_wave, rec_cell, rec_data):
    rows, own_cols = velocity.shape[1:]
    halo = round_up(STEPS * PASSES, SUBLANES)
    window = rows + 2 * halo
    height = round_up(rows + 2 * STEPS * PASSES, SUBLANES)
    nsrc, nrec = src_cell.shape[0], rec_cell.shape[0]
    blocks = NY // LANES
    assert src_wave.shape[1] == 1 and rows % SUBLANES == 0 and rows >= halo
    vmem = pl.BlockSpec(memory_space=pltpu.VMEM)
    return pl.pallas_call(
        functools.partial(kernel, freqs, tiles),
        out_shape=(
            jax.ShapeDtypeStruct((2, 1, 2, rows, NY), jnp.float32),
            jax.ShapeDtypeStruct((STEPS, rows, own_cols), jnp.float32),
        ),
        in_specs=[pl.BlockSpec(memory_space=pltpu.HBM)] * 7,
        out_specs=(vmem, vmem),
        scratch_shapes=[
            pltpu.VMEM((1, nsrc), jnp.int32),
            pltpu.VMEM((nsrc // LANES, LANES), jnp.int32),
            pltpu.VMEM((2, 1, nsrc), jnp.float32),
            pltpu.VMEM((1, nrec), jnp.int32),
            pltpu.VMEM((nrec // LANES, LANES), jnp.int32),
            pltpu.VMEM((2, 1, nrec), jnp.float32),
            pltpu.VMEM((STEPS, window, NY), jnp.float32),
            pltpu.VMEM((PASSES + 1, 4, blocks, window + 2 * SUBLANES, LANES), jnp.float32),
            pltpu.VMEM((2 * blocks * height, 2 * LANES), jnp.float32),
            pltpu.VMEM((STEPS, rows, NY), jnp.float32),
            pltpu.VMEM((STEPS, freqs, rows, own_cols), jnp.float32),
            pltpu.SemaphoreType.DMA((3, freqs, STEPS)),
            pltpu.SemaphoreType.DMA((3, freqs, STEPS)),
            pltpu.SemaphoreType.DMA((STEPS, freqs)),
            pltpu.SemaphoreType.DMA((STEPS, freqs)),
            pltpu.SemaphoreType.DMA((7,)),
        ],
        compiler_params=pltpu.CompilerParams(
            collective_id=0, has_side_effects=True, vmem_limit_bytes=60 * 1024 * 1024
        ),
    )(
        velocity,
        src_cell.reshape(1, -1),
        src_cell.reshape(-1, LANES),
        src_wave,
        rec_cell.reshape(1, -1),
        rec_cell.reshape(-1, LANES),
        rec_data,
    )


def solution(mesh):
    placed = (
        P(None, "tile", "freq"),
        P("shots"),
        P(None, "freq", "shots"),
        P("shots"),
        P(None, "freq", "shots"),
    )
    return jax.shard_map(
        functools.partial(body, mesh.shape["freq"], mesh.shape["tile"]),
        mesh=mesh,
        in_specs=placed,
        out_specs=(P("shots", "freq", None, "tile", None), P("shots", "tile", "freq")),
        check_vma=False,
    )
```

```python
import functools
import math

import jax
import jax.numpy as jnp
from jax import lax
from jax.experimental import pallas as pl
from jax.experimental.pallas import tpu as pltpu
from jax.sharding import PartitionSpec as P

NY = 1024
STEPS = 4
PASSES = 5
LANES = 128
SUBLANES = 8

term_weights = (0.3, 0.25, -0.15, 0.12, -0.1, 0.08)
phase_unit = 0.25
slowest = 1.5

MESH = pl.DeviceIdType.MESH


def round_up(value, unit):
    return -(-value // unit) * unit


def series(angle, largest):
    square = angle * angle
    terms = 1
    while largest ** (2 * terms) / math.factorial(2 * terms) > 1e-9:
        terms += 1
    cos = sin = None
    for n in reversed(range(terms)):
        sign = -1.0 if n % 2 else 1.0
        even, odd = sign / math.factorial(2 * n), sign / math.factorial(2 * n + 1)
        cos = even if cos is None else cos * square + even
        sin = odd if sin is None else sin * square + odd
    return cos, sin * angle


def times(x, y):
    return x[0] * y[0] - x[1] * y[1], x[0] * y[1] + x[1] * y[0]


def double(x):
    twice = x[1] + x[1]
    return 1.0 - twice * x[1], twice * x[0]


def coefficients(kappa, largest):
    e15 = series(kappa * 0.15, largest * 0.15)
    e20 = series(kappa * 0.2, largest * 0.2)
    e30 = double(e15)
    e45 = times(e30, e15)
    e60 = double(e30)
    e80 = times(e60, e20)
    e100 = times(e80, e20)
    return [
        (w * c, w * s) for w, (c, s) in zip(term_weights, (e100, e80, e60, e45, e30, e20))
    ]


def kernel(
    freqs,
    tiles,
    velocity,
    src_cell_in,
    src_wave_in,
    rec_cell_in,
    rec_data_in,
    fields_out,
    image_out,
    src_cell,
    src_wave,
    rec_cell,
    rec_data,
    speed,
    order,
    speed_inside,
    image_inside,
    terms,
    sums,
    partial_image,
    image_in,
    speed_send,
    speed_recv,
    image_send,
    image_recv,
    local,
):
    f = lax.axis_index("freq")
    t = lax.axis_index("tile")
    rows = velocity.shape[1]
    own_cols = velocity.shape[2]
    blocks = NY // LANES
    reach = STEPS * PASSES
    halo = round_up(reach, SUBLANES)
    window = rows + 2 * halo
    pad = SUBLANES
    has_above = t > 0
    has_below = t < tiles - 1

    groups = []
    for z in range(STEPS - 1):
        height = round_up(PASSES * (STEPS - 1 - z), SUBLANES)
        if groups and groups[-1][2] == height:
            groups[-1][1] = z + 1
        else:
            groups.append([z, z + 1, height])

    def other(step):
        return lax.rem(f + step, freqs)

    def columns(owner):
        return pl.ds(pl.multiple_of(owner * own_cols, own_cols), own_cols)

    loads = [
        pltpu.make_async_copy(source, target, local.at[i])
        for i, (source, target) in enumerate(
            (
                (src_cell_in, src_cell),
                (src_wave_in, src_wave),
                (rec_cell_in, rec_cell),
                (rec_data_in, rec_data),
                (velocity, speed.at[:, pl.ds(halo, rows), columns(f)]),
            )
        )
    ]
    for load in loads:
        load.start()

    for b in range(blocks):
        column = lax.broadcasted_iota(jnp.int32, (NY, LANES), 0)
        inner = lax.broadcasted_iota(jnp.int32, (NY, LANES), 1) * blocks + b
        order[:, pl.ds(b * LANES, LANES)] = jnp.where(column == inner, 1.0, 0.0).astype(
            jnp.bfloat16
        )

    def reordered(values, side):
        head = values.astype(jnp.bfloat16)
        rest = (values - head.astype(jnp.float32)).astype(jnp.bfloat16)
        both = lax.dot_general(
            jnp.concatenate([head, rest], axis=0),
            order[...],
            (((1,), (side,)), ((), ())),
            preferred_element_type=jnp.float32,
        )
        return both[: values.shape[0]] + both[values.shape[0] :]

    barrier = pltpu.get_barrier_semaphore()

    def greet(device):
        pl.semaphore_signal(barrier, inc=1, device_id=device, device_id_type=MESH)

    for step in range(1, freqs):
        greet({"freq": other(step)})

    @pl.when(has_above)
    def _():
        for step in range(freqs):
            greet({"freq": other(step), "tile": t - 1})

    @pl.when(has_below)
    def _():
        for step in range(freqs):
            greet({"freq": other(step), "tile": t + 1})

    neighbours = has_above.astype(jnp.int32) + has_below.astype(jnp.int32)
    pl.semaphore_wait(barrier, freqs - 1 + freqs * neighbours)

    def level_copy(owner, target):
        return pltpu.make_async_remote_copy(
            src_ref=velocity,
            dst_ref=speed.at[:, pl.ds(halo, rows), columns(owner)],
            send_sem=speed_send.at[0, target, 0],
            recv_sem=speed_recv.at[0, owner, 0],
            device_id={"freq": target},
            device_id_type=MESH,
        )

    def down_copy(owner, target, g):
        low, high, height = groups[g]
        return pltpu.make_async_remote_copy(
            src_ref=velocity.at[pl.ds(low, high - low), pl.ds(rows - height, height)],
            dst_ref=speed.at[
                pl.ds(low, high - low), pl.ds(halo - height, height), columns(owner)
            ],
            send_sem=speed_send.at[1, target, g],
            recv_sem=speed_recv.at[1, owner, g],
            device_id={"freq": target, "tile": lax.rem(t + 1, tiles)},
            device_id_type=MESH,
        )

    def up_copy(owner, target, g):
        low, high, height = groups[g]
        return pltpu.make_async_remote_copy(
            src_ref=velocity.at[pl.ds(low, high - low), pl.ds(0, height)],
            dst_ref=speed.at[
                pl.ds(low, high - low), pl.ds(halo + rows, height), columns(owner)
            ],
            send_sem=speed_send.at[2, target, g],
            recv_sem=speed_recv.at[2, owner, g],
            device_id={"freq": target, "tile": lax.rem(t + tiles - 1, tiles)},
            device_id_type=MESH,
        )

    for step in range(1, freqs):
        level_copy(f, other(step)).start()

    @pl.when(has_below)
    def _():
        for g in range(len(groups)):
            for step in range(freqs):
                down_copy(f, other(step), g).start()

    @pl.when(has_above)
    def _():
        for g in range(len(groups)):
            for step in range(freqs):
                up_copy(f, other(step), g).start()

    @pl.when(jnp.logical_not(has_above))
    def _():
        speed[:, pl.ds(0, halo), :] = jnp.full((STEPS, halo, NY), 2.0, jnp.float32)

    @pl.when(jnp.logical_not(has_below))
    def _():
        speed[:, pl.ds(halo + rows, halo), :] = jnp.full((STEPS, halo, NY), 2.0, jnp.float32)

    for edge in (0, pad + window):
        terms[:, :, :, pl.ds(edge, pad), :] = jnp.zeros(
            (PASSES + 1, 4, blocks, pad, LANES), jnp.float32
        )
    edge_rows = round_up(halo - reach, SUBLANES)
    for edge in (pad, pad + window - edge_rows):
        if edge_rows:
            terms[0, :, :, pl.ds(edge, edge_rows), :] = jnp.zeros(
                (4, blocks, edge_rows, LANES), jnp.float32
            )

    first_row = t * rows - reach
    height = round_up(rows + 2 * reach, SUBLANES)

    def inject(cells, data, field):
        count = cells.shape[1]
        chunk = math.gcd(count, 1024)
        sums[...] = jnp.zeros_like(sums)

        def add(i, carry):
            part = pl.ds(pl.multiple_of(i * chunk, chunk), chunk)
            cell = cells[:, part]
            row = (cell >> 10) - first_row
            col = cell & (NY - 1)
            inside = (row >= 0) & (row < height)
            place = jnp.where(inside, (col & (blocks - 1)) * height + row, -1)
            lane = col >> (blocks.bit_length() - 1)
            place, lane = place.astype(jnp.int16), lane.astype(jnp.int16)
            at_place = lax.broadcasted_iota(jnp.int16, (blocks * height, chunk), 0) == place
            at_lane = lax.broadcasted_iota(jnp.int16, (LANES, chunk), 0) == lane
            one, zero = jnp.bfloat16(1.0), jnp.bfloat16(0.0)
            spread = []
            for c in range(2):
                value = data[c, :, part]
                head = value.astype(jnp.bfloat16)
                rest = (value - head.astype(jnp.float32)).astype(jnp.bfloat16)
                for piece in (head, rest):
                    spread.append(jnp.where(at_lane, piece, zero))
            one_hot = jnp.where(at_place, one, zero)
            sums[...] += lax.dot_general(
                one_hot,
                jnp.concatenate(spread, axis=0),
                (((1,), (1,)), ((), ())),
                preferred_element_type=jnp.float32,
            )
            return carry

        lax.fori_loop(0, count // chunk, add, 0)
        for c in range(2):
            for b in range(blocks):
                part = pl.ds(b * height, height)
                terms[0, 2 * field + c, b, pl.ds(pad + halo - reach, height), :] = (
                    sums[part, pl.ds(2 * c * LANES, LANES)]
                    + sums[part, pl.ds((2 * c + 1) * LANES, LANES)]
                )

    loads[0].wait()
    loads[1].wait()
    inject(src_cell, src_wave, 0)
    loads[2].wait()
    loads[3].wait()
    inject(rec_cell, rec_data, 1)
    loads[4].wait()

    for step in range(1, freqs):
        level_copy(other(step), other(step)).wait_recv()

    @pl.when(has_above)
    def _():
        for g in range(len(groups)):
            for owner in range(freqs):
                down_copy(owner, owner, g).wait_recv()

    @pl.when(has_below)
    def _():
        for g in range(len(groups)):
            for owner in range(freqs):
                up_copy(owner, owner, g).wait_recv()

    above_grid = jnp.where(has_above, 1.0, 0.0).astype(jnp.float32)
    below_grid = jnp.where(has_below, 1.0, 0.0).astype(jnp.float32)
    lane_index = lax.broadcasted_iota(jnp.int32, (SUBLANES, LANES), 1)
    at_first = lane_index == 0
    at_last = lane_index == LANES - 1
    number = (f + 1).astype(jnp.float32)
    largest = freqs * phase_unit / slowest

    def strips(margin):
        low = (halo - margin) // SUBLANES
        return range(low, round_up(halo + rows + margin, SUBLANES) // SUBLANES)

    def image_copy(z, owner, source):
        return pltpu.make_async_remote_copy(
            src_ref=partial_image.at[z, :, columns(owner)],
            dst_ref=image_in.at[z, source],
            send_sem=image_send.at[z, owner],
            recv_sem=image_recv.at[z, source],
            device_id={"freq": owner},
            device_id_type=MESH,
        )

    spans = [strips(PASSES * (STEPS - 1 - z)) for z in range(STEPS)]
    inner_speed = reordered(
        jnp.concatenate(
            [
                speed[z, pl.ds(span[0] * SUBLANES, len(span) * SUBLANES), :]
                for z, span in enumerate(spans)
            ],
            axis=0,
        ),
        0,
    )
    top = 0
    for z, span in enumerate(spans):
        extent = len(span) * SUBLANES
        for b in range(blocks):
            speed_inside[z, b, pl.ds(span[0] * SUBLANES, extent), :] = inner_speed[
                top : top + extent, b * LANES : (b + 1) * LANES
            ]
        top += extent

    def finish_images(low, high):
        outer = reordered(
            jnp.concatenate(
                [
                    jnp.concatenate([image_inside[z, b] for b in range(blocks)], axis=1)
                    for z in range(low, high)
                ],
                axis=0,
            ),
            1,
        )
        for z in range(low, high):
            partial_image[z] = outer[(z - low) * rows : (z - low + 1) * rows]
            for step in range(1, freqs):
                image_copy(z, other(step), f).start()

    for z in range(STEPS):
        margin = PASSES * (STEPS - 1 - z)

        for k in range(1, PASSES + 1):

            def advance(plane, carry):
                for s in strips(margin + PASSES - k):
                    top = pad + s * SUBLANES
                    twice, tall = [], []
                    for b in range(blocks):
                        here = terms[k - 1, plane, b, pl.ds(top, SUBLANES), :]
                        over = terms[k - 1, plane, b, pl.ds(top - 1, SUBLANES), :]
                        under = terms[k - 1, plane, b, pl.ds(top + 1, SUBLANES), :]
                        twice.append(here + here)
                        tall.append(twice[b] + (over + under))
                    for b in range(blocks):
                        before = tall[b - 1] if b else jnp.where(at_first, 0.0, pltpu.roll(tall[blocks - 1], 1, 1))
                        after = tall[b + 1] if b < blocks - 1 else jnp.where(at_last, 0.0, pltpu.roll(tall[0], LANES - 1, 1))
                        wide = (tall[b] + tall[b]) + (before + after)
                        if k == 1:
                            new = 0.125 * wide - 0.5 * twice[b]
                        else:
                            new = (0.25 * wide - twice[b]) - terms[
                                k - 2, plane, b, pl.ds(top, SUBLANES), :
                            ]
                        if s * SUBLANES < halo:
                            new = new * above_grid
                        elif s * SUBLANES >= halo + rows:
                            new = new * below_grid
                        terms[k, plane, b, pl.ds(top, SUBLANES), :] = new
                return carry

            lax.fori_loop(0, 4, advance, 0)

        def combine(b, carry):
            for s in strips(margin):
                top = pad + s * SUBLANES
                kappa = (number * phase_unit) / speed_inside[z, b, pl.ds(s * SUBLANES, SUBLANES), :]
                total = [None] * 4
                for k, (real, imag) in enumerate(coefficients(kappa, largest)):
                    u = [terms[k, p, b, pl.ds(top, SUBLANES), :] for p in range(4)]
                    new = (
                        real * u[0] - imag * u[1],
                        real * u[1] + imag * u[0],
                        real * u[2] + imag * u[3],
                        real * u[3] - imag * u[2],
                    )
                    total = [n if o is None else o + n for o, n in zip(total, new)]
                own = s * SUBLANES - halo
                inside = 0 <= own < rows
                for p in range(4):
                    terms[0, p, b, pl.ds(top, SUBLANES), :] = total[p]
                if inside:
                    image_inside[z, b, pl.ds(own, SUBLANES), :] = (
                        total[0] * total[2] + total[1] * total[3]
                    )
            return carry

        lax.fori_loop(0, blocks, combine, 0)
        if z == STEPS - 2:
            finish_images(0, STEPS - 1)
        elif z == STEPS - 1:
            finish_images(STEPS - 1, STEPS)

    own_rows = pl.ds(pad + halo, rows)
    outer_fields = reordered(
        jnp.concatenate(
            [
                jnp.concatenate([terms[0, p, b, own_rows, :] for b in range(blocks)], axis=1)
                for p in range(4)
            ],
            axis=0,
        ),
        1,
    )
    for p in range(4):
        fields_out[p // 2, 0, p % 2] = outer_fields[p * rows : (p + 1) * rows]

    for z in range(STEPS):
        whole = partial_image[z, :, columns(f)]
        for step in range(1, freqs):
            image_copy(z, f, other(step)).wait_recv()
            whole = whole + image_in[z, other(step)]
        image_out[z] = whole

    for z in range(STEPS):
        for step in range(1, freqs):
            image_copy(z, other(step), f).wait_send()
    for step in range(1, freqs):
        level_copy(f, other(step)).wait_send()

    @pl.when(has_below)
    def _():
        for g in range(len(groups)):
            for step in range(freqs):
                down_copy(f, other(step), g).wait_send()

    @pl.when(has_above)
    def _():
        for g in range(len(groups)):
            for step in range(freqs):
                up_copy(f, other(step), g).wait_send()


def body(freqs, tiles, velocity, src_cell, src_wave, rec_cell, rec_data):
    rows, own_cols = velocity.shape[1:]
    halo = round_up(STEPS * PASSES, SUBLANES)
    window = rows + 2 * halo
    height = round_up(rows + 2 * STEPS * PASSES, SUBLANES)
    nsrc, nrec = src_cell.shape[0], rec_cell.shape[0]
    blocks = NY // LANES
    assert src_wave.shape[1] == 1 and rows % SUBLANES == 0 and rows >= halo
    vmem = pl.BlockSpec(memory_space=pltpu.VMEM)
    return pl.pallas_call(
        functools.partial(kernel, freqs, tiles),
        out_shape=(
            jax.ShapeDtypeStruct((2, 1, 2, rows, NY), jnp.float32),
            jax.ShapeDtypeStruct((STEPS, rows, own_cols), jnp.float32),
        ),
        in_specs=[pl.BlockSpec(memory_space=pltpu.HBM)] * 5,
        out_specs=(vmem, vmem),
        scratch_shapes=[
            pltpu.VMEM((1, nsrc), jnp.int32),
            pltpu.VMEM((2, 1, nsrc), jnp.float32),
            pltpu.VMEM((1, nrec), jnp.int32),
            pltpu.VMEM((2, 1, nrec), jnp.float32),
            pltpu.VMEM((STEPS, window, NY), jnp.float32),
            pltpu.VMEM((NY, NY), jnp.bfloat16),
            pltpu.VMEM((STEPS, blocks, window, LANES), jnp.float32),
            pltpu.VMEM((STEPS, blocks, rows, LANES), jnp.float32),
            pltpu.VMEM((PASSES + 1, 4, blocks, window + 2 * SUBLANES, LANES), jnp.float32),
            pltpu.VMEM((blocks * height, 4 * LANES), jnp.float32),
            pltpu.VMEM((STEPS, rows, NY), jnp.float32),
            pltpu.VMEM((STEPS, freqs, rows, own_cols), jnp.float32),
            pltpu.SemaphoreType.DMA((3, freqs, STEPS)),
            pltpu.SemaphoreType.DMA((3, freqs, STEPS)),
            pltpu.SemaphoreType.DMA((STEPS, freqs)),
            pltpu.SemaphoreType.DMA((STEPS, freqs)),
            pltpu.SemaphoreType.DMA((5,)),
        ],
        compiler_params=pltpu.CompilerParams(
            collective_id=0, has_side_effects=True, vmem_limit_bytes=60 * 1024 * 1024
        ),
    )(velocity, src_cell.reshape(1, -1), src_wave, rec_cell.reshape(1, -1), rec_data)


def solution(mesh):
    placed = (
        P(None, "tile", "freq"),
        P("shots"),
        P(None, "freq", "shots"),
        P("shots"),
        P(None, "freq", "shots"),
    )
    return jax.shard_map(
        functools.partial(body, mesh.shape["freq"], mesh.shape["tile"]),
        mesh=mesh,
        in_specs=placed,
        out_specs=(P("shots", "freq", None, "tile", None), P("shots", "tile", "freq")),
        check_vma=False,
    )
```

```python
import functools
import math

import jax
import jax.numpy as jnp
from jax import lax
from jax.experimental import pallas as pl
from jax.experimental.pallas import tpu as pltpu
from jax.sharding import PartitionSpec as P

NY = 1024
STEPS = 4
PASSES = 5
LANES = 128
SUBLANES = 8

term_weights = (0.3, 0.25, -0.15, 0.12, -0.1, 0.08)
phase_unit = 0.25
slowest = 1.5

MESH = pl.DeviceIdType.MESH


def round_up(value, unit):
    return -(-value // unit) * unit


def series(angle, largest):
    square = angle * angle
    terms = 1
    while largest ** (2 * terms) / math.factorial(2 * terms) > 1e-9:
        terms += 1
    cos = sin = None
    for n in reversed(range(terms)):
        sign = -1.0 if n % 2 else 1.0
        even, odd = sign / math.factorial(2 * n), sign / math.factorial(2 * n + 1)
        cos = even if cos is None else cos * square + even
        sin = odd if sin is None else sin * square + odd
    return cos, sin * angle


def times(x, y):
    return x[0] * y[0] - x[1] * y[1], x[0] * y[1] + x[1] * y[0]


def double(x):
    twice = x[1] + x[1]
    return 1.0 - twice * x[1], twice * x[0]


def coefficients(kappa, largest):
    e15 = series(kappa * 0.15, largest * 0.15)
    e20 = series(kappa * 0.2, largest * 0.2)
    e30 = double(e15)
    e45 = times(e30, e15)
    e60 = double(e30)
    e80 = times(e60, e20)
    e100 = times(e80, e20)
    return [
        (w * c, w * s) for w, (c, s) in zip(term_weights, (e100, e80, e60, e45, e30, e20))
    ]


def kernel(
    freqs,
    tiles,
    velocity,
    src_cell_in,
    src_wave_in,
    rec_cell_in,
    rec_data_in,
    fields_out,
    image_out,
    src_cell,
    src_wave,
    rec_cell,
    rec_data,
    speed,
    order,
    speed_inside,
    image_inside,
    terms,
    sums,
    partial_image,
    image_in,
    speed_send,
    speed_recv,
    image_send,
    image_recv,
    local,
):
    f = lax.axis_index("freq")
    t = lax.axis_index("tile")
    rows = velocity.shape[1]
    own_cols = velocity.shape[2]
    blocks = NY // LANES
    reach = STEPS * PASSES
    halo = round_up(reach, SUBLANES)
    window = rows + 2 * halo
    pad = SUBLANES
    has_above = t > 0
    has_below = t < tiles - 1

    groups = []
    for z in range(STEPS - 1):
        height = round_up(PASSES * (STEPS - 1 - z), SUBLANES)
        if groups and groups[-1][2] == height:
            groups[-1][1] = z + 1
        else:
            groups.append([z, z + 1, height])

    def other(step):
        return lax.rem(f + step, freqs)

    def columns(owner):
        return pl.ds(pl.multiple_of(owner * own_cols, own_cols), own_cols)

    loads = [
        pltpu.make_async_copy(source, target, local.at[i])
        for i, (source, target) in enumerate(
            (
                (src_cell_in, src_cell),
                (src_wave_in, src_wave),
                (rec_cell_in, rec_cell),
                (rec_data_in, rec_data),
                (velocity, speed.at[:, pl.ds(halo, rows), columns(f)]),
            )
        )
    ]
    for load in loads:
        load.start()

    for b in range(blocks):
        column = lax.broadcasted_iota(jnp.int32, (NY, LANES), 0)
        inner = lax.broadcasted_iota(jnp.int32, (NY, LANES), 1) * blocks + b
        order[:, pl.ds(b * LANES, LANES)] = jnp.where(column == inner, 1.0, 0.0).astype(
            jnp.bfloat16
        )

    def reordered(values, side):
        head = values.astype(jnp.bfloat16)
        rest = (values - head.astype(jnp.float32)).astype(jnp.bfloat16)
        both = lax.dot_general(
            jnp.concatenate([head, rest], axis=0),
            order[...],
            (((1,), (side,)), ((), ())),
            preferred_element_type=jnp.float32,
        )
        return both[: values.shape[0]] + both[values.shape[0] :]

    barrier = pltpu.get_barrier_semaphore()

    def greet(device):
        pl.semaphore_signal(barrier, inc=1, device_id=device, device_id_type=MESH)

    for step in range(1, freqs):
        greet({"freq": other(step)})

    @pl.when(has_above)
    def _():
        for step in range(freqs):
            greet({"freq": other(step), "tile": t - 1})

    @pl.when(has_below)
    def _():
        for step in range(freqs):
            greet({"freq": other(step), "tile": t + 1})

    neighbours = has_above.astype(jnp.int32) + has_below.astype(jnp.int32)
    pl.semaphore_wait(barrier, freqs - 1 + freqs * neighbours)

    def level_copy(owner, target):
        return pltpu.make_async_remote_copy(
            src_ref=velocity,
            dst_ref=speed.at[:, pl.ds(halo, rows), columns(owner)],
            send_sem=speed_send.at[0, target, 0],
            recv_sem=speed_recv.at[0, owner, 0],
            device_id={"freq": target},
            device_id_type=MESH,
        )

    def down_copy(owner, target, g):
        low, high, height = groups[g]
        return pltpu.make_async_remote_copy(
            src_ref=velocity.at[pl.ds(low, high - low), pl.ds(rows - height, height)],
            dst_ref=speed.at[
                pl.ds(low, high - low), pl.ds(halo - height, height), columns(owner)
            ],
            send_sem=speed_send.at[1, target, g],
            recv_sem=speed_recv.at[1, owner, g],
            device_id={"freq": target, "tile": lax.rem(t + 1, tiles)},
            device_id_type=MESH,
        )

    def up_copy(owner, target, g):
        low, high, height = groups[g]
        return pltpu.make_async_remote_copy(
            src_ref=velocity.at[pl.ds(low, high - low), pl.ds(0, height)],
            dst_ref=speed.at[
                pl.ds(low, high - low), pl.ds(halo + rows, height), columns(owner)
            ],
            send_sem=speed_send.at[2, target, g],
            recv_sem=speed_recv.at[2, owner, g],
            device_id={"freq": target, "tile": lax.rem(t + tiles - 1, tiles)},
            device_id_type=MESH,
        )

    for step in range(1, freqs):
        level_copy(f, other(step)).start()

    @pl.when(has_below)
    def _():
        for g in range(len(groups)):
            for step in range(freqs):
                down_copy(f, other(step), g).start()

    @pl.when(has_above)
    def _():
        for g in range(len(groups)):
            for step in range(freqs):
                up_copy(f, other(step), g).start()

    @pl.when(jnp.logical_not(has_above))
    def _():
        speed[:, pl.ds(0, halo), :] = jnp.full((STEPS, halo, NY), 2.0, jnp.float32)

    @pl.when(jnp.logical_not(has_below))
    def _():
        speed[:, pl.ds(halo + rows, halo), :] = jnp.full((STEPS, halo, NY), 2.0, jnp.float32)

    for edge in (0, pad + window):
        terms[:, :, :, pl.ds(edge, pad), :] = jnp.zeros(
            (PASSES + 1, 4, blocks, pad, LANES), jnp.float32
        )
    edge_rows = round_up(halo - reach, SUBLANES)
    for edge in (pad, pad + window - edge_rows):
        if edge_rows:
            terms[0, :, :, pl.ds(edge, edge_rows), :] = jnp.zeros(
                (4, blocks, edge_rows, LANES), jnp.float32
            )

    first_row = t * rows - reach
    height = round_up(rows + 2 * reach, SUBLANES)

    def inject(cells, data, field):
        count = cells.shape[1]
        chunk = math.gcd(count, 1024)
        sums[...] = jnp.zeros_like(sums)

        def add(i, carry):
            part = pl.ds(pl.multiple_of(i * chunk, chunk), chunk)
            cell = cells[:, part]
            row = (cell >> 10) - first_row
            col = cell & (NY - 1)
            inside = (row >= 0) & (row < height)
            place = jnp.where(inside, (col & (blocks - 1)) * height + row, -1)
            lane = col >> (blocks.bit_length() - 1)
            place, lane = place.astype(jnp.int16), lane.astype(jnp.int16)
            at_place = lax.broadcasted_iota(jnp.int16, (blocks * height, chunk), 0) == place
            at_lane = lax.broadcasted_iota(jnp.int16, (LANES, chunk), 0) == lane
            one, zero = jnp.bfloat16(1.0), jnp.bfloat16(0.0)
            spread = []
            for c in range(2):
                value = data[c, :, part]
                head = value.astype(jnp.bfloat16)
                rest = (value - head.astype(jnp.float32)).astype(jnp.bfloat16)
                for piece in (head, rest):
                    spread.append(jnp.where(at_lane, piece, zero))
            one_hot = jnp.where(at_place, one, zero)
            sums[...] += lax.dot_general(
                one_hot,
                jnp.concatenate(spread, axis=0),
                (((1,), (1,)), ((), ())),
                preferred_element_type=jnp.float32,
            )
            return carry

        lax.fori_loop(0, count // chunk, add, 0)
        for c in range(2):
            for b in range(blocks):
                part = pl.ds(b * height, height)
                terms[0, 2 * field + c, b, pl.ds(pad + halo - reach, height), :] = (
                    sums[part, pl.ds(2 * c * LANES, LANES)]
                    + sums[part, pl.ds((2 * c + 1) * LANES, LANES)]
                )

    loads[0].wait()
    loads[1].wait()
    inject(src_cell, src_wave, 0)
    loads[2].wait()
    loads[3].wait()
    inject(rec_cell, rec_data, 1)
    loads[4].wait()

    for step in range(1, freqs):
        level_copy(other(step), other(step)).wait_recv()

    @pl.when(has_above)
    def _():
        for g in range(len(groups)):
            for owner in range(freqs):
                down_copy(owner, owner, g).wait_recv()

    @pl.when(has_below)
    def _():
        for g in range(len(groups)):
            for owner in range(freqs):
                up_copy(owner, owner, g).wait_recv()

    above_grid = jnp.where(has_above, 1.0, 0.0).astype(jnp.float32)
    below_grid = jnp.where(has_below, 1.0, 0.0).astype(jnp.float32)
    lane_index = lax.broadcasted_iota(jnp.int32, (SUBLANES, LANES), 1)
    at_first = lane_index == 0
    at_last = lane_index == LANES - 1
    number = (f + 1).astype(jnp.float32)
    largest = freqs * phase_unit / slowest

    def strips(margin):
        low = (halo - margin) // SUBLANES
        return range(low, round_up(halo + rows + margin, SUBLANES) // SUBLANES)

    def image_copy(z, owner, source):
        return pltpu.make_async_remote_copy(
            src_ref=partial_image.at[z, :, columns(owner)],
            dst_ref=image_in.at[z, source],
            send_sem=image_send.at[z, owner],
            recv_sem=image_recv.at[z, source],
            device_id={"freq": owner},
            device_id_type=MESH,
        )

    spans = [strips(PASSES * (STEPS - 1 - z)) for z in range(STEPS)]
    inner_speed = reordered(
        jnp.concatenate(
            [
                speed[z, pl.ds(span[0] * SUBLANES, len(span) * SUBLANES), :]
                for z, span in enumerate(spans)
            ],
            axis=0,
        ),
        0,
    )
    top = 0
    for z, span in enumerate(spans):
        extent = len(span) * SUBLANES
        for b in range(blocks):
            speed_inside[z, b, pl.ds(span[0] * SUBLANES, extent), :] = inner_speed[
                top : top + extent, b * LANES : (b + 1) * LANES
            ]
        top += extent

    def finish_images(low, high):
        outer = reordered(
            jnp.concatenate(
                [
                    jnp.concatenate([image_inside[z, b] for b in range(blocks)], axis=1)
                    for z in range(low, high)
                ],
                axis=0,
            ),
            1,
        )
        for z in range(low, high):
            partial_image[z] = outer[(z - low) * rows : (z - low + 1) * rows]
            for step in range(1, freqs):
                image_copy(z, other(step), f).start()

    for z in range(STEPS):
        margin = PASSES * (STEPS - 1 - z)

        for k in range(1, PASSES + 1):

            def advance(plane, carry):
                for s in strips(margin + PASSES - k):
                    top = pad + s * SUBLANES
                    twice, tall = [], []
                    for b in range(blocks):
                        here = terms[k - 1, plane, b, pl.ds(top, SUBLANES), :]
                        over = terms[k - 1, plane, b, pl.ds(top - 1, SUBLANES), :]
                        under = terms[k - 1, plane, b, pl.ds(top + 1, SUBLANES), :]
                        twice.append(here + here)
                        tall.append(twice[b] + (over + under))
                    for b in range(blocks):
                        before = tall[b - 1] if b else jnp.where(at_first, 0.0, pltpu.roll(tall[blocks - 1], 1, 1))
                        after = tall[b + 1] if b < blocks - 1 else jnp.where(at_last, 0.0, pltpu.roll(tall[0], LANES - 1, 1))
                        wide = (tall[b] + tall[b]) + (before + after)
                        if k == 1:
                            new = 0.125 * wide - 0.5 * twice[b]
                        else:
                            new = (0.25 * wide - twice[b]) - terms[
                                k - 2, plane, b, pl.ds(top, SUBLANES), :
                            ]
                        if s * SUBLANES < halo:
                            new = new * above_grid
                        elif s * SUBLANES >= halo + rows:
                            new = new * below_grid
                        terms[k, plane, b, pl.ds(top, SUBLANES), :] = new
                return carry

            lax.fori_loop(0, 4, advance, 0, unroll=2)

        def combine(b, carry):
            for s in strips(margin):
                top = pad + s * SUBLANES
                kappa = (number * phase_unit) / speed_inside[z, b, pl.ds(s * SUBLANES, SUBLANES), :]
                total = [None] * 4
                for k, (real, imag) in enumerate(coefficients(kappa, largest)):
                    u = [terms[k, p, b, pl.ds(top, SUBLANES), :] for p in range(4)]
                    new = (
                        real * u[0] - imag * u[1],
                        real * u[1] + imag * u[0],
                        real * u[2] + imag * u[3],
                        real * u[3] - imag * u[2],
                    )
                    total = [n if o is None else o + n for o, n in zip(total, new)]
                own = s * SUBLANES - halo
                inside = 0 <= own < rows
                for p in range(4):
                    terms[0, p, b, pl.ds(top, SUBLANES), :] = total[p]
                if inside:
                    image_inside[z, b, pl.ds(own, SUBLANES), :] = (
                        total[0] * total[2] + total[1] * total[3]
                    )
            return carry

        lax.fori_loop(0, blocks, combine, 0, unroll=2)
        if z == STEPS - 2:
            finish_images(0, STEPS - 1)
        elif z == STEPS - 1:
            finish_images(STEPS - 1, STEPS)

    own_rows = pl.ds(pad + halo, rows)
    outer_fields = reordered(
        jnp.concatenate(
            [
                jnp.concatenate([terms[0, p, b, own_rows, :] for b in range(blocks)], axis=1)
                for p in range(4)
            ],
            axis=0,
        ),
        1,
    )
    for p in range(4):
        fields_out[p // 2, 0, p % 2] = outer_fields[p * rows : (p + 1) * rows]

    for z in range(STEPS):
        whole = partial_image[z, :, columns(f)]
        for step in range(1, freqs):
            image_copy(z, f, other(step)).wait_recv()
            whole = whole + image_in[z, other(step)]
        image_out[z] = whole

    for z in range(STEPS):
        for step in range(1, freqs):
            image_copy(z, other(step), f).wait_send()
    for step in range(1, freqs):
        level_copy(f, other(step)).wait_send()

    @pl.when(has_below)
    def _():
        for g in range(len(groups)):
            for step in range(freqs):
                down_copy(f, other(step), g).wait_send()

    @pl.when(has_above)
    def _():
        for g in range(len(groups)):
            for step in range(freqs):
                up_copy(f, other(step), g).wait_send()


def body(freqs, tiles, velocity, src_cell, src_wave, rec_cell, rec_data):
    rows, own_cols = velocity.shape[1:]
    halo = round_up(STEPS * PASSES, SUBLANES)
    window = rows + 2 * halo
    height = round_up(rows + 2 * STEPS * PASSES, SUBLANES)
    nsrc, nrec = src_cell.shape[0], rec_cell.shape[0]
    blocks = NY // LANES
    assert src_wave.shape[1] == 1 and rows % SUBLANES == 0 and rows >= halo
    vmem = pl.BlockSpec(memory_space=pltpu.VMEM)
    return pl.pallas_call(
        functools.partial(kernel, freqs, tiles),
        out_shape=(
            jax.ShapeDtypeStruct((2, 1, 2, rows, NY), jnp.float32),
            jax.ShapeDtypeStruct((STEPS, rows, own_cols), jnp.float32),
        ),
        in_specs=[pl.BlockSpec(memory_space=pltpu.HBM)] * 5,
        out_specs=(vmem, vmem),
        scratch_shapes=[
            pltpu.VMEM((1, nsrc), jnp.int32),
            pltpu.VMEM((2, 1, nsrc), jnp.float32),
            pltpu.VMEM((1, nrec), jnp.int32),
            pltpu.VMEM((2, 1, nrec), jnp.float32),
            pltpu.VMEM((STEPS, window, NY), jnp.float32),
            pltpu.VMEM((NY, NY), jnp.bfloat16),
            pltpu.VMEM((STEPS, blocks, window, LANES), jnp.float32),
            pltpu.VMEM((STEPS, blocks, rows, LANES), jnp.float32),
            pltpu.VMEM((PASSES + 1, 4, blocks, window + 2 * SUBLANES, LANES), jnp.float32),
            pltpu.VMEM((blocks * height, 4 * LANES), jnp.float32),
            pltpu.VMEM((STEPS, rows, NY), jnp.float32),
            pltpu.VMEM((STEPS, freqs, rows, own_cols), jnp.float32),
            pltpu.SemaphoreType.DMA((3, freqs, STEPS)),
            pltpu.SemaphoreType.DMA((3, freqs, STEPS)),
            pltpu.SemaphoreType.DMA((STEPS, freqs)),
            pltpu.SemaphoreType.DMA((STEPS, freqs)),
            pltpu.SemaphoreType.DMA((5,)),
        ],
        compiler_params=pltpu.CompilerParams(
            collective_id=0, has_side_effects=True, vmem_limit_bytes=60 * 1024 * 1024
        ),
    )(velocity, src_cell.reshape(1, -1), src_wave, rec_cell.reshape(1, -1), rec_data)


def solution(mesh):
    placed = (
        P(None, "tile", "freq"),
        P("shots"),
        P(None, "freq", "shots"),
        P("shots"),
        P(None, "freq", "shots"),
    )
    return jax.shard_map(
        functools.partial(body, mesh.shape["freq"], mesh.shape["tile"]),
        mesh=mesh,
        in_specs=placed,
        out_specs=(P("shots", "freq", None, "tile", None), P("shots", "tile", "freq")),
        check_vma=False,
    )
```
